512 devices in a mesh: tile: 128 (over y, z, core), pair: 4 (over x).
Axes of the slice: x: 4, y: 8, z: 8, core: 2. Of those that a mesh axis runs over, the one named last changes fastest.
Arguments:
- amplitudes: bfloat16 [48, 512, 800], P(None, ('tile', 'pair')), may hold values from -6 to 6
- integrals: bfloat16 [768, 200, 1600], P('tile', None, 'pair'), may hold values from -0.1875 to 0.1875
- tile_column: int32 [768], P('tile'), may hold values from 0 to 47
- block_symmetry: int32 [128], P('tile'), may hold values from 0 to 3
Outputs:
- residual: bfloat16 [512, 128, 1600], P(('tile', 'pair'))
The draws below stay inside these ranges and needn't reach their ends.
All inputs are finite; a program needn't handle non-finite values.
Results may differ from the reference program's by a relative error of at most 0.001.
Values may be sent and summed in bfloat16 or wider, within the bound.
No kernel may reach another device: no remote copies, remote signals or barrier semaphores. Data moves between devices by JAX's collectives and lax.ppermute only.
A program may use at most 64 MiB of HBM per device.

```python
import jax
import jax.numpy as jnp
from jax import lax

NVIR = 800
IRREP = 200
C_WINDOW = 48
TILES_DEV = 6
A_BLOCK = 8
PAIRS = 512
TILES = 768
N_TILE = 128


def touch_ends(result, own_key, least, largest):
    spot = [jax.random.randint(jax.random.fold_in(own_key, axis), (), 0, length) for axis, length in enumerate(result.shape)]
    longest = result.shape.index(max(result.shape))
    neighbour = spot[:longest] + [(spot[longest] + 1) % result.shape[longest]] + spot[longest + 1:]
    return result.at[tuple(spot)].set(least).at[tuple(neighbour)].set(largest)


def levels(own_key, dims, cuts, least, largest):
    def one(axis_at, shards_of):
        steps = jax.random.uniform(jax.random.fold_in(jax.random.fold_in(own_key, 6), axis_at), (shards_of,), jnp.float32, least / len(cuts), largest / len(cuts))
        return jnp.repeat(jnp.exp(steps), dims[axis_at] // shards_of).reshape((-1,) + (1,) * (len(dims) - axis_at - 1))

    gain = one(*cuts[0])
    for cut in cuts[1:]:
        gain = gain * one(*cut)
    return gain


def noise(rng, dims, spread, reach, shards=(), kind=jnp.bfloat16):
    gain = levels(rng, dims, shards, -0.22, 0.18) if shards else 1.0
    result = jax.random.normal(rng, dims, jnp.float32) * spread * gain
    return jnp.minimum(jnp.maximum(result, -reach), reach).astype(kind)


def setup_inputs(seed: int = 0) -> dict:
    key_list = jax.random.split(jax.random.key(seed), 5)
    return {
        "amplitudes": noise(key_list[0], (C_WINDOW, PAIRS, NVIR), 1.0, 6.0, ((1, 512),)),
        "integrals": noise(key_list[1], (TILES, IRREP, A_BLOCK * IRREP), (TILES_DEV * IRREP) ** -0.5, 0.1875, ((0, 128), (2, 4))),
        "tile_column": touch_ends(jax.random.randint(key_list[2], (TILES,), 0, C_WINDOW), jax.random.fold_in(key_list[2], 1), 0, C_WINDOW - 1).astype(jnp.int32),
        "block_symmetry": touch_ends(jax.random.randint(key_list[3], (N_TILE,), 0, 4), jax.random.fold_in(key_list[3], 1), 0, 3).astype(jnp.int32),
    }


def reference(amplitudes, integrals, tile_column, block_symmetry):
    quarters = amplitudes.reshape(C_WINDOW, PAIRS, 4, IRREP)

    def owner_block(owner):
        columns_used = lax.dynamic_slice_in_dim(tile_column, owner * TILES_DEV, TILES_DEV)
        symmetry = lax.dynamic_slice_in_dim(block_symmetry, owner, 1)[0]
        wanted = jnp.bitwise_xor(symmetry, columns_used // (C_WINDOW // 4)).astype(jnp.int32)
        tiles = lax.dynamic_slice_in_dim(integrals, owner * TILES_DEV, TILES_DEV)
        summed = jnp.zeros((PAIRS, A_BLOCK * IRREP), jnp.float32)
        for slot in range(TILES_DEV):
            piece = quarters[columns_used[slot], :, wanted[slot], :]
            summed = summed + jnp.dot(piece, tiles[slot], preferred_element_type=jnp.float32)
        return summed.astype(jnp.bfloat16)

    stacked = lax.map(owner_block, jnp.arange(N_TILE, dtype=jnp.int32))
    return jnp.transpose(stacked, (1, 0, 2))
```

```python
import functools

import jax
import jax.numpy as jnp
from jax import lax
from jax.experimental import pallas as pl
from jax.experimental.pallas import tpu as pltpu
from jax.sharding import Mesh, PartitionSpec as P

LANES = 128
BF16 = jnp.bfloat16
F32 = jnp.float32

HEAD = 128
MIDDLE = 64
LAST = 8


def pack_kernel(w_ref, out_ref):
    slots, width, columns = w_ref.shape
    depth = slots * width
    slabs = columns // LANES
    left = columns - slabs * LANES

    def ordered(lo, hi):
        heads = [w_ref[k, :HEAD, lo:hi] for k in range(slots)]
        middles = [w_ref[k, HEAD : HEAD + MIDDLE, lo:hi] for k in range(slots)]
        ends = [w_ref[k, HEAD + MIDDLE :, lo:hi].astype(F32) for k in range(slots)]
        return heads + middles + [jnp.concatenate(ends, axis=0).astype(BF16)]

    for s in range(slabs):
        at = s * depth
        for part in ordered(s * LANES, (s + 1) * LANES):
            out_ref[at : at + part.shape[0], :] = part
            at += part.shape[0]
    narrow = jnp.concatenate(ordered(slabs * LANES, columns), axis=0)
    eye = (
        lax.broadcasted_iota(jnp.int32, (left, left), 0) == lax.broadcasted_iota(jnp.int32, (left, left), 1)
    ).astype(BF16)
    turned = lax.dot_general(eye, narrow, (((1,), (1,)), ((), ())), preferred_element_type=F32)
    chunks = -(-depth // LANES)
    turned = jnp.concatenate([turned, jnp.zeros((left, chunks * LANES - depth), F32)], axis=1).astype(BF16)
    for j in range(chunks):
        at = slabs * depth + j * left
        out_ref[at : at + left, :] = turned[:, j * LANES : (j + 1) * LANES]


def pack(integrals):
    slots, width, columns = integrals.shape
    slabs = columns // LANES
    left = columns - slabs * LANES
    rows = slabs * slots * width + -(-slots * width // LANES) * left
    return pl.pallas_call(
        pack_kernel,
        out_shape=jax.ShapeDtypeStruct((rows, LANES), BF16),
        in_specs=[pl.BlockSpec(memory_space=pltpu.VMEM)],
        out_specs=pl.BlockSpec(memory_space=pltpu.VMEM),
        compiler_params=pltpu.CompilerParams(vmem_limit_bytes=24 << 20),
        cost_estimate=pl.CostEstimate(flops=0, bytes_accessed=4 * rows * LANES, transcendentals=0),
        name="pack_integrals",
    )(integrals)


def select_kernel(slots, core_ref, own_ref, other_ref, wanted_ref, out_ref):
    window, virtuals = own_ref.shape
    width = virtuals // 4
    peers = wanted_ref.shape[0]
    first = core_ref[0] == 0
    own = own_ref[...].astype(F32)
    other = other_ref[...].astype(F32)
    rows = [jnp.where(first, own, other), jnp.where(first, other, own)]
    blank = jnp.zeros((4 * window, 2 * LANES - width), F32)
    quarters = [jnp.concatenate([row[:, h * width : (h + 1) * width] for h in range(4)], axis=0) for row in rows]
    table = jnp.concatenate([quarters[0], blank, quarters[1], blank], axis=1).astype(BF16)
    places = lax.broadcasted_iota(jnp.int32, (peers, 4 * window), 1)
    wanted = wanted_ref[...]
    pieces = []
    for k in range(slots):
        chosen = (places == wanted[:, k : k + 1]).astype(F32).astype(BF16)
        pieces.append(jnp.dot(chosen, table, preferred_element_type=F32))
    chunks = out_ref.shape[0] // 2
    for r in range(2):
        base = r * 2 * LANES
        for k in range(slots):
            out_ref[r * chunks + k] = pieces[k][:, base : base + LANES].astype(BF16)
        for j in range(slots // 2):
            lo, hi = base + HEAD, base + HEAD + MIDDLE
            pair = [pieces[2 * j][:, lo:hi], pieces[2 * j + 1][:, lo:hi]]
            out_ref[r * chunks + slots + j] = jnp.concatenate(pair, axis=1).astype(BF16)
        lo = base + HEAD + MIDDLE
        ends = [pieces[k][:, lo : lo + LAST] for k in range(slots)]
        ends.append(jnp.zeros((peers, LANES - slots * LAST), F32))
        out_ref[r * chunks + chunks - 1] = jnp.concatenate(ends, axis=1).astype(BF16)


def select(slots, core, own, other, wanted):
    peers = wanted.shape[0]
    chunks = slots + slots // 2 + 1
    whole = pl.BlockSpec(memory_space=pltpu.VMEM)
    return pl.pallas_call(
        functools.partial(select_kernel, slots),
        out_shape=jax.ShapeDtypeStruct((2 * chunks, peers, LANES), BF16),
        in_specs=[pl.BlockSpec(memory_space=pltpu.SMEM), whole, whole, whole],
        out_specs=whole,
        compiler_params=pltpu.CompilerParams(vmem_limit_bytes=24 << 20),
        name="select_pieces",
    )(core, own, other, wanted)


def contract_kernel(depth, columns, a_ref, w_ref, out_ref, tails):
    p = pl.program_id(0)
    chunks = a_ref.shape[0] // 2
    slabs = columns // LANES
    left = columns - slabs * LANES
    halves = [jnp.concatenate([a_ref[r * chunks + j] for j in range(chunks)], axis=1) for r in range(2)]
    a = jnp.concatenate(halves, axis=0)
    w = jnp.concatenate([w_ref[0, s * depth : (s + 1) * depth, :] for s in range(slabs)], axis=1)
    product = jnp.dot(a[:, :depth], w, preferred_element_type=F32).astype(BF16)
    for s in range(slabs):
        out_ref[slabs * p + s] = product[:, s * LANES : (s + 1) * LANES]
    base = slabs * depth
    parts = [w_ref[0, base + j * left : base + (j + 1) * left, :] for j in range(chunks)]

    @pl.when(p == 0)
    def _():
        tails[...] = jnp.zeros_like(tails)

    tails[pl.ds(pl.multiple_of(p * left, left), left), :] = jnp.concatenate(parts, axis=1)

    @pl.when(p == pl.num_programs(0) - 1)
    def _():
        last = lax.dot_general(a, tails[...], (((1,), (1,)), ((), ())), preferred_element_type=F32)
        out_ref[out_ref.shape[0] - 1] = last.astype(BF16)


def contract(depth, columns, arrived, gathered):
    ring, rows, _ = gathered.shape
    chunks2, peers, _ = arrived.shape
    slabs = columns // LANES
    outs = ring * slabs + 1
    return pl.pallas_call(
        functools.partial(contract_kernel, depth, columns),
        grid=(ring,),
        out_shape=jax.ShapeDtypeStruct((outs, 2 * peers, LANES), BF16),
        in_specs=[
            pl.BlockSpec((chunks2, peers, LANES), lambda p: (0, 0, 0)),
            pl.BlockSpec((1, rows, LANES), lambda p: (p, 0, 0)),
        ],
        out_specs=pl.BlockSpec((outs, 2 * peers, LANES), lambda p: (0, 0, 0)),
        scratch_shapes=[pltpu.VMEM((LANES, chunks2 // 2 * LANES), BF16)],
        compiler_params=pltpu.CompilerParams(vmem_limit_bytes=24 << 20),
        name="contract",
    )(arrived, gathered)


def place_kernel(columns, r_ref, out_ref):
    count, blocks, _ = r_ref.shape
    half = blocks // 2
    slabs = columns // LANES
    left = columns - slabs * LANES
    came = lax.broadcasted_iota(jnp.int32, (blocks, blocks), 0)
    goes = lax.broadcasted_iota(jnp.int32, (blocks, blocks), 1)
    order = jnp.where(came < half, 2 * came, 2 * (came - half) + 1)
    turn = (order == goes).astype(F32).astype(BF16)
    for j in range(count):
        block = lax.dot_general(r_ref[j], turn, (((0,), (0,)), ((), ())), preferred_element_type=F32).astype(BF16)
        if j < count - 1:
            at = j // slabs * columns + j % slabs * LANES
            out_ref[at : at + LANES, :] = block
        else:
            for p in range((count - 1) // slabs):
                at = p * columns + slabs * LANES
                out_ref[at : at + left, :] = block[p * left : (p + 1) * left]


def place(columns, received):
    count, blocks, _ = received.shape
    ring = (count - 1) // (columns // LANES)
    whole = pl.BlockSpec(memory_space=pltpu.VMEM)
    return pl.pallas_call(
        functools.partial(place_kernel, columns),
        out_shape=jax.ShapeDtypeStruct((ring * columns, blocks), BF16),
        in_specs=[whole],
        out_specs=whole,
        compiler_params=pltpu.CompilerParams(vmem_limit_bytes=24 << 20),
        name="place_rows",
    )(received)


def local(amplitudes, integrals, tile_column, block_symmetry):
    window, _, virtuals = amplitudes.shape
    slots, width, columns = integrals.shape
    depth = slots * width
    peers = lax.axis_size("y") * lax.axis_size("z")
    core = lax.axis_index("core")

    packed = pack(integrals)
    gathered = lax.all_gather(packed, "pair", axis=0, tiled=False)

    own = amplitudes.reshape(window, virtuals)
    other = lax.ppermute(own, "core", [(0, 1), (1, 0)])
    symmetry = jnp.bitwise_xor(block_symmetry[0], tile_column // (window // 4))
    wanted = jnp.zeros((LANES,), jnp.int32).at[:slots].set(symmetry * window + tile_column)
    asked = lax.all_to_all(jnp.broadcast_to(wanted, (peers, LANES)), ("y", "z"), 0, 0, tiled=True)

    outgoing = select(slots, core.reshape(1), own, other, asked)
    arrived = lax.all_to_all(outgoing, ("y", "z"), 1, 1, tiled=True)
    rows = contract(depth, columns, arrived, gathered)
    received = lax.all_to_all(rows, ("core", "y", "z"), 1, 1, tiled=True)
    return place(columns, received).T[None]


def solution(mesh):
    sizes = {2: (1, 1), 8: (2, 2), 128: (8, 8)}[mesh.shape["tile"]]
    fine = Mesh(mesh.devices.reshape(*sizes, 2, mesh.shape["pair"]), ("y", "z", "core", "pair"))
    tile = ("y", "z", "core")
    in_specs = (P(None, (*tile, "pair"), None), P(tile, None, "pair"), P(tile), P(tile))
    out_specs = P((*tile, "pair"), None, None)
    return jax.shard_map(local, mesh=fine, in_specs=in_specs, out_specs=out_specs, check_vma=False)
```

```python
import functools

import jax
import jax.numpy as jnp
from jax import lax
from jax.experimental import pallas as pl
from jax.experimental.pallas import tpu as pltpu
from jax.sharding import Mesh, PartitionSpec as P

LANES = 128
BF16 = jnp.bfloat16
F32 = jnp.float32

HEAD = 128
MIDDLE = 64
LAST = 8

def pack_kernel(w_ref, out_ref):
    slots, width, columns = w_ref.shape
    depth = slots * width
    slabs = columns // LANES
    left = columns - slabs * LANES

    def ordered(lo, hi):
        heads = [w_ref[k, :HEAD, lo:hi] for k in range(slots)]
        middles = [w_ref[k, HEAD : HEAD + MIDDLE, lo:hi] for k in range(slots)]
        ends = [w_ref[k, HEAD + MIDDLE :, lo:hi].astype(F32) for k in range(slots)]
        return heads + middles + [jnp.concatenate(ends, axis=0).astype(BF16)]

    for s in range(slabs):
        at = s * depth
        for part in ordered(s * LANES, (s + 1) * LANES):
            out_ref[at : at + part.shape[0], :] = part
            at += part.shape[0]
    narrow = jnp.concatenate(ordered(slabs * LANES, columns), axis=0)
    eye = (
        lax.broadcasted_iota(jnp.int32, (left, left), 0) == lax.broadcasted_iota(jnp.int32, (left, left), 1)
    ).astype(BF16)
    turned = lax.dot_general(eye, narrow, (((1,), (1,)), ((), ())), preferred_element_type=F32)
    chunks = -(-depth // LANES)
    turned = jnp.concatenate([turned, jnp.zeros((left, chunks * LANES - depth), F32)], axis=1).astype(BF16)
    for j in range(chunks):
        at = slabs * depth + j * left
        out_ref[at : at + left, :] = turned[:, j * LANES : (j + 1) * LANES]


def pack(integrals):
    slots, width, columns = integrals.shape
    slabs = columns // LANES
    left = columns - slabs * LANES
    depth = slots * width
    rows = slabs * depth + -(-depth // LANES) * left
    whole = pl.BlockSpec(memory_space=pltpu.VMEM)
    return pl.pallas_call(
        pack_kernel,
        out_shape=jax.ShapeDtypeStruct((rows, LANES), BF16),
        in_specs=[whole],
        out_specs=whole,
        compiler_params=pltpu.CompilerParams(vmem_limit_bytes=24 << 20),
        name="pack_integrals",
    )(integrals)


def ask_kernel(window, column_ref, symmetry_ref, out_ref):
    peers, tile, _ = out_ref.shape
    lanes = lax.broadcasted_iota(jnp.int32, (tile, LANES), 1)
    row = jnp.zeros((tile, LANES), F32)
    for k in range(column_ref.shape[0]):
        column = column_ref[k]
        irrep = sum((column >= h * (window // 4)).astype(jnp.int32) for h in (1, 2, 3))
        place = jnp.bitwise_xor(symmetry_ref[0], irrep) * window + column
        row = jnp.where(lanes == k, place.astype(F32), row)
    row = row.astype(BF16)
    for j in range(peers):
        out_ref[j] = row


def ask(window, peers, tile_column, block_symmetry):
    scalars = pl.BlockSpec(memory_space=pltpu.SMEM)
    return pl.pallas_call(
        functools.partial(ask_kernel, window),
        out_shape=jax.ShapeDtypeStruct((peers, 8, LANES), BF16),
        in_specs=[scalars, scalars],
        out_specs=pl.BlockSpec(memory_space=pltpu.VMEM),
        name="ask_pieces",
    )(tile_column, block_symmetry)


def table_kernel(core_ref, own_ref, other_ref, out_ref):
    window, virtuals = own_ref.shape
    width = virtuals // 4
    first = core_ref[0] == 0
    own = own_ref[...].astype(F32)
    other = other_ref[...].astype(F32)
    rows = [jnp.where(first, own, other), jnp.where(first, other, own)]
    blank = jnp.zeros((4 * window, 2 * LANES - width), F32)
    quarters = [jnp.concatenate([row[:, h * width : (h + 1) * width] for h in range(4)], axis=0) for row in rows]
    out_ref[...] = jnp.concatenate([quarters[0], blank, quarters[1], blank], axis=1).astype(BF16)


def build_table(core, own, other):
    whole = pl.BlockSpec(memory_space=pltpu.VMEM)
    return pl.pallas_call(
        table_kernel,
        out_shape=jax.ShapeDtypeStruct((4 * own.shape[0], 4 * LANES), BF16),
        in_specs=[pl.BlockSpec(memory_space=pltpu.SMEM), whole, whole],
        out_specs=whole,
        compiler_params=pltpu.CompilerParams(vmem_limit_bytes=24 << 20),
        name="build_table",
    )(core, own, other)


def select_kernel(slots, table_ref, asked_ref, out_ref):
    peers = asked_ref.shape[0]
    table = table_ref[...]
    wanted = asked_ref[...].astype(F32)[:, 0, :].astype(jnp.int32)
    places = lax.broadcasted_iota(jnp.int32, (peers, table.shape[0]), 1)
    pieces = []
    for k in range(slots):
        chosen = (places == wanted[:, k : k + 1]).astype(F32).astype(BF16)
        pieces.append(jnp.dot(chosen, table, preferred_element_type=F32))
    chunks = out_ref.shape[0] // 2
    for r in range(2):
        base = r * 2 * LANES
        for k in range(slots):
            out_ref[r * chunks + k] = pieces[k][:, base : base + LANES].astype(BF16)
        for j in range(slots // 2):
            lo, hi = base + HEAD, base + HEAD + MIDDLE
            pair = [pieces[2 * j][:, lo:hi], pieces[2 * j + 1][:, lo:hi]]
            out_ref[r * chunks + slots + j] = jnp.concatenate(pair, axis=1).astype(BF16)
        lo = base + HEAD + MIDDLE
        ends = [pieces[k][:, lo : lo + LAST] for k in range(slots)]
        ends.append(jnp.zeros((peers, LANES - slots * LAST), F32))
        out_ref[r * chunks + chunks - 1] = jnp.concatenate(ends, axis=1).astype(BF16)


def select(slots, table, asked):
    peers = asked.shape[0]
    chunks = slots + slots // 2 + 1
    whole = pl.BlockSpec(memory_space=pltpu.VMEM)
    return pl.pallas_call(
        functools.partial(select_kernel, slots),
        out_shape=jax.ShapeDtypeStruct((2 * chunks, peers, LANES), BF16),
        in_specs=[whole, whole],
        out_specs=whole,
        compiler_params=pltpu.CompilerParams(vmem_limit_bytes=24 << 20),
        name="select_pieces",
    )(table, asked)


def contract_kernel(depth, columns, me_ref, a_ref, *refs):
    parts, out_ref, tails = refs[:-2], refs[-2], refs[-1]
    ring = len(parts)
    chunks = a_ref.shape[0] // 2
    slabs = columns // LANES
    left = columns - slabs * LANES
    halves = [jnp.concatenate([a_ref[r * chunks + j] for j in range(chunks)], axis=1) for r in range(2)]
    a = jnp.concatenate(halves, axis=0)
    tails[...] = jnp.zeros_like(tails)
    for step, part in enumerate(parts):
        p = lax.rem(me_ref[0] + step, ring)
        wide = jnp.concatenate([part[s * depth : (s + 1) * depth, :] for s in range(slabs)], axis=1)
        product = jnp.dot(a[:, :depth], wide, preferred_element_type=F32).astype(BF16)
        for s in range(slabs):
            out_ref[slabs * p + s] = product[:, s * LANES : (s + 1) * LANES]
        narrow = [part[at : at + left, :] for at in range(slabs * depth, part.shape[0], left)]
        tails[pl.ds(pl.multiple_of(p * left, left), left), :] = jnp.concatenate(narrow, axis=1)
    last = lax.dot_general(a, tails[...], (((1,), (1,)), ((), ())), preferred_element_type=F32)
    out_ref[out_ref.shape[0] - 1] = last.astype(BF16)


def contract(depth, columns, me, arrived, parts):
    ring = len(parts)
    chunks2, peers, _ = arrived.shape
    outs = ring * (columns // LANES) + 1
    whole = pl.BlockSpec(memory_space=pltpu.VMEM)
    return pl.pallas_call(
        functools.partial(contract_kernel, depth, columns),
        out_shape=jax.ShapeDtypeStruct((outs, 2 * peers, LANES), BF16),
        in_specs=[pl.BlockSpec(memory_space=pltpu.SMEM)] + [whole] * (1 + ring),
        out_specs=whole,
        scratch_shapes=[pltpu.VMEM((LANES, chunks2 // 2 * LANES), BF16)],
        compiler_params=pltpu.CompilerParams(vmem_limit_bytes=24 << 20),
        name="contract",
    )(me, arrived, *parts)


def place_kernel(columns, r_ref, out_ref):
    count, blocks, _ = r_ref.shape
    half = blocks // 2
    slabs = columns // LANES
    left = columns - slabs * LANES
    came = lax.broadcasted_iota(jnp.int32, (blocks, blocks), 0)
    goes = lax.broadcasted_iota(jnp.int32, (blocks, blocks), 1)
    order = jnp.where(came < half, 2 * came, 2 * (came - half) + 1)
    turn = (order == goes).astype(F32).astype(BF16)
    for j in range(count):
        block = lax.dot_general(r_ref[j], turn, (((0,), (0,)), ((), ())), preferred_element_type=F32).astype(BF16)
        if j < count - 1:
            at = j // slabs * columns + j % slabs * LANES
            out_ref[at : at + LANES, :] = block
        else:
            for p in range((count - 1) // slabs):
                at = p * columns + slabs * LANES
                out_ref[at : at + left, :] = block[p * left : (p + 1) * left]


def place(columns, received):
    count, blocks, _ = received.shape
    ring = (count - 1) // (columns // LANES)
    whole = pl.BlockSpec(memory_space=pltpu.VMEM)
    return pl.pallas_call(
        functools.partial(place_kernel, columns),
        out_shape=jax.ShapeDtypeStruct((ring * columns, blocks), BF16),
        in_specs=[whole],
        out_specs=whole,
        compiler_params=pltpu.CompilerParams(vmem_limit_bytes=24 << 20),
        name="place_rows",
    )(received)


def local(amplitudes, integrals, tile_column, block_symmetry):
    window, _, virtuals = amplitudes.shape
    slots, width, columns = integrals.shape
    depth = slots * width
    ring = lax.axis_size("pair")
    peers = lax.axis_size("y") * lax.axis_size("z")

    packed = pack(integrals)
    asked = lax.all_to_all(ask(window, peers, tile_column, block_symmetry), ("y", "z"), 0, 0, tiled=True)

    own = amplitudes.reshape(window, virtuals)
    other = lax.ppermute(own, "core", [(0, 1), (1, 0)])
    table = build_table(lax.axis_index("core").reshape(1), own, other)
    parts = [packed]
    parts += [lax.ppermute(packed, "pair", [((i + k) % ring, i) for i in range(ring)]) for k in range(1, ring)]

    outgoing = select(slots, table, asked)
    arrived = lax.all_to_all(outgoing, ("y", "z"), 1, 1, tiled=True)
    rows = contract(depth, columns, lax.axis_index("pair").reshape(1), arrived, parts)
    received = lax.all_to_all(rows, ("core", "y", "z"), 1, 1, tiled=True)
    return place(columns, received).T[None]


def solution(mesh):
    sizes = {2: (1, 1), 8: (2, 2), 128: (8, 8)}[mesh.shape["tile"]]
    fine = Mesh(mesh.devices.reshape(*sizes, 2, mesh.shape["pair"]), ("y", "z", "core", "pair"))
    tile = ("y", "z", "core")
    in_specs = (P(None, (*tile, "pair"), None), P(tile, None, "pair"), P(tile), P(tile))
    out_specs = P((*tile, "pair"), None, None)
    return jax.shard_map(local, mesh=fine, in_specs=in_specs, out_specs=out_specs, check_vma=False)
```

```python
import functools
import math

import jax
import jax.numpy as jnp
from jax import lax
from jax.experimental import pallas as pl
from jax.experimental.pallas import tpu as pltpu
from jax.sharding import Mesh, PartitionSpec as P

LANES = 128
BF16 = jnp.bfloat16
F32 = jnp.float32

HEAD = 128
MIDDLE = 64
LAST = 8

TILE = ("y4", "y2", "y1", "z4", "z2", "z1", "core")
SERVED = ("z1", "z2", "z4", "y1", "y2", "y4")

def pack_kernel(window, w_hbm, column_hbm, symmetry_hbm, out_ref, ask_ref, w_ref, column_ref, symmetry_ref, arrivals):
    slots, width, columns = w_ref.shape
    scalars = [
        pltpu.make_async_copy(column_hbm, column_ref, arrivals.at[slots]),
        pltpu.make_async_copy(symmetry_hbm, symmetry_ref, arrivals.at[slots + 1]),
    ]
    tiles = [pltpu.make_async_copy(w_hbm.at[k], w_ref.at[k], arrivals.at[k]) for k in range(slots)]
    for copy in scalars + tiles:
        copy.start()

    for copy in scalars:
        copy.wait()
    peers, tile, _ = ask_ref.shape
    lanes = lax.broadcasted_iota(jnp.int32, (tile, LANES), 1)
    row = jnp.zeros((tile, LANES), F32)
    for k in range(slots):
        column = column_ref[k]
        irrep = sum((column >= h * (window // 4)).astype(jnp.int32) for h in (1, 2, 3))
        place = jnp.bitwise_xor(symmetry_ref[0], irrep) * window + column
        row = jnp.where(lanes == k, place.astype(F32), row)
    row = row.astype(BF16)
    for j in range(peers):
        ask_ref[j] = row

    depth = slots * width
    slabs = columns // LANES
    left = columns - slabs * LANES
    for k in range(slots):
        tiles[k].wait()
        for s in range(slabs):
            lo, hi = s * LANES, (s + 1) * LANES
            at = s * depth + k * HEAD
            out_ref[at : at + HEAD, :] = w_ref[k, :HEAD, lo:hi]
            at = s * depth + slots * HEAD + k * MIDDLE
            out_ref[at : at + MIDDLE, :] = w_ref[k, HEAD : HEAD + MIDDLE, lo:hi]

    def ends(lo, hi):
        return jnp.concatenate([w_ref[k, HEAD + MIDDLE :, lo:hi].astype(F32) for k in range(slots)], axis=0).astype(BF16)

    for s in range(slabs):
        at = s * depth + slots * (HEAD + MIDDLE)
        out_ref[at : at + slots * LAST, :] = ends(s * LANES, (s + 1) * LANES)
    lo, hi = slabs * LANES, columns
    narrow = [w_ref[k, :HEAD, lo:hi] for k in range(slots)]
    narrow += [w_ref[k, HEAD : HEAD + MIDDLE, lo:hi] for k in range(slots)]
    narrow = jnp.concatenate(narrow + [ends(lo, hi)], axis=0)
    eye = (
        lax.broadcasted_iota(jnp.int32, (left, left), 0) == lax.broadcasted_iota(jnp.int32, (left, left), 1)
    ).astype(BF16)
    turned = lax.dot_general(eye, narrow, (((1,), (1,)), ((), ())), preferred_element_type=F32)
    chunks = -(-depth // LANES)
    turned = jnp.concatenate([turned, jnp.zeros((left, chunks * LANES - depth), F32)], axis=1).astype(BF16)
    for j in range(chunks):
        at = slabs * depth + j * left
        out_ref[at : at + left, :] = turned[:, j * LANES : (j + 1) * LANES]


def pack(window, peers, integrals, tile_column, block_symmetry):
    slots, width, columns = integrals.shape
    slabs = columns // LANES
    left = columns - slabs * LANES
    depth = slots * width
    rows = slabs * depth + -(-depth // LANES) * left
    anywhere = pl.BlockSpec(memory_space=pl.ANY)
    whole = pl.BlockSpec(memory_space=pltpu.VMEM)
    return pl.pallas_call(
        functools.partial(pack_kernel, window),
        out_shape=[
            jax.ShapeDtypeStruct((rows, LANES), BF16),
            jax.ShapeDtypeStruct((peers, 8, LANES), BF16),
        ],
        in_specs=[anywhere, anywhere, anywhere],
        out_specs=[whole, whole],
        scratch_shapes=[
            pltpu.VMEM(integrals.shape, BF16),
            pltpu.SMEM(tile_column.shape, jnp.int32),
            pltpu.SMEM(block_symmetry.shape, jnp.int32),
            pltpu.SemaphoreType.DMA((slots + 2,)),
        ],
        compiler_params=pltpu.CompilerParams(vmem_limit_bytes=60 << 20),
        name="pack_integrals",
    )(integrals, tile_column, block_symmetry)


def table_kernel(core_ref, own_ref, other_ref, out_ref):
    window, virtuals = own_ref.shape
    width = virtuals // 4
    first = core_ref[0] == 0
    own = own_ref[...].astype(F32)
    other = other_ref[...].astype(F32)
    rows = [jnp.where(first, own, other), jnp.where(first, other, own)]
    blank = jnp.zeros((4 * window, 2 * LANES - width), F32)
    quarters = [jnp.concatenate([row[:, h * width : (h + 1) * width] for h in range(4)], axis=0) for row in rows]
    out_ref[...] = jnp.concatenate([quarters[0], blank, quarters[1], blank], axis=1).astype(BF16)


def build_table(core, own, other):
    whole = pl.BlockSpec(memory_space=pltpu.VMEM)
    return pl.pallas_call(
        table_kernel,
        out_shape=jax.ShapeDtypeStruct((4 * own.shape[0], 4 * LANES), BF16),
        in_specs=[pl.BlockSpec(memory_space=pltpu.SMEM), whole, whole],
        out_specs=whole,
        compiler_params=pltpu.CompilerParams(vmem_limit_bytes=24 << 20),
        name="build_table",
    )(core, own, other)


def select_kernel(slots, table_ref, asked_ref, out_ref):
    peers = asked_ref.shape[0]
    table = table_ref[...]
    wanted = asked_ref[...].astype(F32)[:, 0, :].astype(jnp.int32)
    places = lax.broadcasted_iota(jnp.int32, (peers, table.shape[0]), 1)
    pieces = []
    for k in range(slots):
        chosen = (places == wanted[:, k : k + 1]).astype(F32).astype(BF16)
        pieces.append(jnp.dot(chosen, table, preferred_element_type=F32))
    chunks = out_ref.shape[0] // 2
    for r in range(2):
        base = r * 2 * LANES
        for k in range(slots):
            out_ref[r * chunks + k] = pieces[k][:, base : base + LANES].astype(BF16)
        for j in range(slots // 2):
            lo, hi = base + HEAD, base + HEAD + MIDDLE
            pair = [pieces[2 * j][:, lo:hi], pieces[2 * j + 1][:, lo:hi]]
            out_ref[r * chunks + slots + j] = jnp.concatenate(pair, axis=1).astype(BF16)
        lo = base + HEAD + MIDDLE
        ends = [pieces[k][:, lo : lo + LAST] for k in range(slots)]
        ends.append(jnp.zeros((peers, LANES - slots * LAST), F32))
        out_ref[r * chunks + chunks - 1] = jnp.concatenate(ends, axis=1).astype(BF16)


def select(slots, table, asked):
    peers = asked.shape[0]
    chunks = slots + slots // 2 + 1
    whole = pl.BlockSpec(memory_space=pltpu.VMEM)
    return pl.pallas_call(
        functools.partial(select_kernel, slots),
        out_shape=jax.ShapeDtypeStruct((2 * chunks, peers, LANES), BF16),
        in_specs=[whole, whole],
        out_specs=whole,
        compiler_params=pltpu.CompilerParams(vmem_limit_bytes=24 << 20),
        name="select_pieces",
    )(table, asked)


def contract_kernel(depth, columns, me_ref, a_ref, *refs):
    parts, out_ref, tails = refs[:-2], refs[-2], refs[-1]
    ring = len(parts)
    chunks = a_ref.shape[0] // 2
    slabs = columns // LANES
    left = columns - slabs * LANES
    halves = [jnp.concatenate([a_ref[r * chunks + j] for j in range(chunks)], axis=1) for r in range(2)]
    a = jnp.concatenate(halves, axis=0)
    tails[...] = jnp.zeros_like(tails)
    for step, part in enumerate(parts):
        p = jnp.bitwise_xor(me_ref[0], (0, *(1, 2, 3))[step])
        wide = jnp.concatenate([part[s * depth : (s + 1) * depth, :] for s in range(slabs)], axis=1)
        product = jnp.dot(a[:, :depth], wide, preferred_element_type=F32).astype(BF16)
        for s in range(slabs):
            out_ref[slabs * p + s] = product[:, s * LANES : (s + 1) * LANES]
        narrow = [part[at : at + left, :] for at in range(slabs * depth, part.shape[0], left)]
        tails[pl.ds(pl.multiple_of(p * left, left), left), :] = jnp.concatenate(narrow, axis=1)
    last = lax.dot_general(a, tails[...], (((1,), (1,)), ((), ())), preferred_element_type=F32)
    out_ref[out_ref.shape[0] - 1] = last.astype(BF16)


def contract(depth, columns, me, arrived, parts):
    ring = len(parts)
    chunks2, peers, _ = arrived.shape
    outs = ring * (columns // LANES) + 1
    whole = pl.BlockSpec(memory_space=pltpu.VMEM)
    return pl.pallas_call(
        functools.partial(contract_kernel, depth, columns),
        out_shape=jax.ShapeDtypeStruct((outs, 2 * peers, LANES), BF16),
        in_specs=[pl.BlockSpec(memory_space=pltpu.SMEM)] + [whole] * (1 + ring),
        out_specs=whole,
        scratch_shapes=[pltpu.VMEM((LANES, chunks2 // 2 * LANES), BF16)],
        compiler_params=pltpu.CompilerParams(vmem_limit_bytes=24 << 20),
        name="contract",
    )(me, arrived, *parts)


def place_kernel(columns, sizes, r_ref, out_ref):
    count, blocks, _ = r_ref.shape
    slabs = columns // LANES
    left = columns - slabs * LANES
    came = lax.broadcasted_iota(jnp.int32, (blocks, blocks), 0)
    goes = lax.broadcasted_iota(jnp.int32, (blocks, blocks), 1)
    order, rest = jnp.zeros_like(came), came
    for axis in reversed(("core", *SERVED)):
        order += rest % sizes[axis] * math.prod(sizes[a] for a in TILE[TILE.index(axis) + 1 :])
        rest = rest // sizes[axis]
    turn = (order == goes).astype(F32).astype(BF16)
    for j in range(count):
        block = lax.dot_general(r_ref[j], turn, (((0,), (0,)), ((), ())), preferred_element_type=F32).astype(BF16)
        if j < count - 1:
            at = j // slabs * columns + j % slabs * LANES
            out_ref[at : at + LANES, :] = block
        else:
            for p in range((count - 1) // slabs):
                at = p * columns + slabs * LANES
                out_ref[at : at + left, :] = block[p * left : (p + 1) * left]


def place(columns, sizes, received):
    count, blocks, _ = received.shape
    ring = (count - 1) // (columns // LANES)
    whole = pl.BlockSpec(memory_space=pltpu.VMEM)
    return pl.pallas_call(
        functools.partial(place_kernel, columns, sizes),
        out_shape=jax.ShapeDtypeStruct((ring * columns, blocks), BF16),
        in_specs=[whole],
        out_specs=whole,
        compiler_params=pltpu.CompilerParams(vmem_limit_bytes=24 << 20),
        name="place_rows",
    )(received)


def local(amplitudes, integrals, tile_column, block_symmetry):
    window, _, virtuals = amplitudes.shape
    slots, width, columns = integrals.shape
    depth = slots * width
    ring = lax.axis_size("pair")
    sizes = {axis: lax.axis_size(axis) for axis in TILE}
    peers = math.prod(sizes[axis] for axis in SERVED)

    packed, wanted = pack(window, peers, integrals, tile_column, block_symmetry)
    asked = lax.all_to_all(wanted, SERVED, 0, 0, tiled=True)
    own = amplitudes.reshape(window, virtuals)
    other = lax.ppermute(own, "core", [(0, 1), (1, 0)])
    table = build_table(lax.axis_index("core").reshape(1), own, other)
    parts = [packed]
    parts += [lax.ppermute(packed, "pair", [(i ^ k, i) for i in range(ring)]) for k in (1, 2, 3)]

    outgoing = select(slots, table, asked)
    arrived = lax.all_to_all(outgoing, SERVED, 1, 1, tiled=True)
    rows = contract(depth, columns, lax.axis_index("pair").reshape(1), arrived, parts)
    received = lax.all_to_all(rows, ("core", *SERVED), 1, 1, tiled=True)
    return place(columns, sizes, received).T[None]


def solution(mesh):
    cut = {8: (1, 1, 2, 1, 1, 2, 2), 16: (1, 2, 2, 1, 1, 2, 2), 128: (2,) * 7}[mesh.shape["tile"]]
    fine = Mesh(mesh.devices.reshape(*cut, mesh.shape["pair"]), (*TILE, "pair"))
    in_specs = (P(None, (*TILE, "pair"), None), P(TILE, None, "pair"), P(TILE), P(TILE))
    out_specs = P((*TILE, "pair"), None, None)
    return jax.shard_map(local, mesh=fine, in_specs=in_specs, out_specs=out_specs, check_vma=False)
```

```python
import functools
import math

import jax
import jax.numpy as jnp
from jax import lax
from jax.experimental import pallas as pl
from jax.experimental.pallas import tpu as pltpu
from jax.sharding import Mesh, PartitionSpec as P

LANES = 128
BF16 = jnp.bfloat16
F32 = jnp.float32

HEAD = 128
MIDDLE = 64
LAST = 8

TILE = ("y4", "y2", "y1", "z4", "z2", "z1", "core")
SERVED = ("y1", "y2", "y4", "z1", "z2", "z4")

PLACES = (0, 1, 2, 3)


def pack_kernel(window, w_hbm, column_hbm, symmetry_hbm, out_hbm, ask_hbm, w_ref, column_ref, symmetry_ref, out_ref, ask_ref, arrivals, departures):
    slots, width, columns = w_ref.shape
    scalars = [
        pltpu.make_async_copy(column_hbm, column_ref, arrivals.at[slots]),
        pltpu.make_async_copy(symmetry_hbm, symmetry_ref, arrivals.at[slots + 1]),
    ]
    tiles = [pltpu.make_async_copy(w_hbm.at[k], w_ref.at[k], arrivals.at[k]) for k in range(slots)]
    for copy in scalars + tiles:
        copy.start()

    for copy in scalars:
        copy.wait()
    peers, tile, _ = ask_ref.shape
    lanes = lax.broadcasted_iota(jnp.int32, (tile, LANES), 1)
    row = jnp.zeros((tile, LANES), F32)
    for k in range(slots):
        column = column_ref[k]
        irrep = sum((column >= h * (window // 4)).astype(jnp.int32) for h in (1, 2, 3))
        place = jnp.bitwise_xor(symmetry_ref[0], irrep) * window + column
        row = jnp.where(lanes == k, place.astype(F32), row)
    row = row.astype(BF16)
    for j in range(peers):
        ask_ref[j] = row
    leaving = [pltpu.make_async_copy(ask_ref, ask_hbm, departures.at[0])]
    leaving[0].start()

    depth = slots * width
    slabs = columns // LANES
    left = columns - slabs * LANES
    for k in range(slots):
        tiles[k].wait()
        for s in range(slabs):
            lo, hi = s * LANES, (s + 1) * LANES
            at = s * depth + k * HEAD
            out_ref[at : at + HEAD, :] = w_ref[k, :HEAD, lo:hi]
            at = s * depth + slots * HEAD + k * MIDDLE
            out_ref[at : at + MIDDLE, :] = w_ref[k, HEAD : HEAD + MIDDLE, lo:hi]

    def ends(lo, hi):
        return jnp.concatenate([w_ref[k, HEAD + MIDDLE :, lo:hi].astype(F32) for k in range(slots)], axis=0).astype(BF16)

    for s in range(slabs):
        at = s * depth + slots * (HEAD + MIDDLE)
        out_ref[at : at + slots * LAST, :] = ends(s * LANES, (s + 1) * LANES)
        rows = pl.ds(s * depth, depth)
        leaving.append(pltpu.make_async_copy(out_ref.at[rows], out_hbm.at[rows], departures.at[1 + s]))
        leaving[-1].start()
    lo, hi = slabs * LANES, columns
    narrow = [w_ref[k, :HEAD, lo:hi] for k in range(slots)]
    narrow += [w_ref[k, HEAD : HEAD + MIDDLE, lo:hi] for k in range(slots)]
    narrow = jnp.concatenate(narrow + [ends(lo, hi)], axis=0)
    eye = (
        lax.broadcasted_iota(jnp.int32, (left, left), 0) == lax.broadcasted_iota(jnp.int32, (left, left), 1)
    ).astype(BF16)
    turned = lax.dot_general(eye, narrow, (((1,), (1,)), ((), ())), preferred_element_type=F32)
    chunks = -(-depth // LANES)
    turned = jnp.concatenate([turned, jnp.zeros((left, chunks * LANES - depth), F32)], axis=1).astype(BF16)
    for j in range(chunks):
        at = slabs * depth + j * left
        out_ref[at : at + left, :] = turned[:, j * LANES : (j + 1) * LANES]
    rows = pl.ds(slabs * depth, chunks * left)
    leaving.append(pltpu.make_async_copy(out_ref.at[rows], out_hbm.at[rows], departures.at[1 + slabs]))
    leaving[-1].start()
    for copy in leaving:
        copy.wait()


def pack(window, peers, integrals, tile_column, block_symmetry):
    slots, width, columns = integrals.shape
    slabs = columns // LANES
    left = columns - slabs * LANES
    depth = slots * width
    rows = slabs * depth + -(-depth // LANES) * left
    anywhere = pl.BlockSpec(memory_space=pl.ANY)
    return pl.pallas_call(
        functools.partial(pack_kernel, window),
        out_shape=[
            jax.ShapeDtypeStruct((rows, LANES), BF16),
            jax.ShapeDtypeStruct((peers, 8, LANES), BF16),
        ],
        in_specs=[anywhere, anywhere, anywhere],
        out_specs=[anywhere, anywhere],
        scratch_shapes=[
            pltpu.VMEM(integrals.shape, BF16),
            pltpu.SMEM(tile_column.shape, jnp.int32),
            pltpu.SMEM(block_symmetry.shape, jnp.int32),
            pltpu.VMEM((rows, LANES), BF16),
            pltpu.VMEM((peers, 8, LANES), BF16),
            pltpu.SemaphoreType.DMA((slots + 2,)),
            pltpu.SemaphoreType.DMA((slabs + 2,)),
        ],
        compiler_params=pltpu.CompilerParams(vmem_limit_bytes=60 << 20),
        name="pack_integrals",
    )(integrals, tile_column, block_symmetry)


def table_kernel(core_ref, own_ref, other_ref, out_ref):
    window, virtuals = own_ref.shape
    width = virtuals // 4
    first = core_ref[0] == 0
    own = own_ref[...].astype(F32)
    other = other_ref[...].astype(F32)
    rows = [jnp.where(first, own, other), jnp.where(first, other, own)]
    blank = jnp.zeros((4 * window, 2 * LANES - width), F32)
    quarters = [jnp.concatenate([row[:, h * width : (h + 1) * width] for h in range(4)], axis=0) for row in rows]
    out_ref[...] = jnp.concatenate([quarters[0], blank, quarters[1], blank], axis=1).astype(BF16)


def build_table(core, own, other):
    whole = pl.BlockSpec(memory_space=pltpu.VMEM)
    return pl.pallas_call(
        table_kernel,
        out_shape=jax.ShapeDtypeStruct((4 * own.shape[0], 4 * LANES), BF16),
        in_specs=[pl.BlockSpec(memory_space=pltpu.SMEM), whole, whole],
        out_specs=whole,
        compiler_params=pltpu.CompilerParams(vmem_limit_bytes=24 << 20),
        name="build_table",
    )(core, own, other)


def select_kernel(slots, table_ref, asked_ref, out_hbm, rows, narrow, departures):
    peers = asked_ref.shape[0]
    table = table_ref[...]
    wanted = asked_ref[...].astype(F32)[:, 0, :].astype(jnp.int32)
    places = lax.broadcasted_iota(jnp.int32, (peers, table.shape[0]), 1)
    pieces = []
    for k in range(slots):
        chosen = (places == wanted[:, k : k + 1]).astype(F32).astype(BF16)
        pieces.append(jnp.dot(chosen, table, preferred_element_type=F32))
    chunks = slots + slots // 2 + 1
    for r in range(2):
        base = r * 2 * LANES
        for k in range(slots):
            rows[:, r * chunks + k, :] = pieces[k][:, base : base + LANES]
        for j in range(slots // 2):
            lo, hi = base + HEAD, base + HEAD + MIDDLE
            pair = [pieces[2 * j][:, lo:hi], pieces[2 * j + 1][:, lo:hi]]
            rows[:, r * chunks + slots + j, :] = jnp.concatenate(pair, axis=1)
        lo = base + HEAD + MIDDLE
        ends = [pieces[k][:, lo : lo + LAST] for k in range(slots)]
        ends.append(jnp.zeros((peers, LANES - slots * LAST), F32))
        rows[:, r * chunks + chunks - 1, :] = jnp.concatenate(ends, axis=1)
    count = departures.shape[0]
    leaving = []
    for k in range(count):
        group = pl.ds(k * (peers // count), peers // count)
        narrow[group] = rows[group].astype(BF16)
        leaving.append(pltpu.make_async_copy(narrow.at[group], out_hbm.at[group], departures.at[k]))
        leaving[-1].start()
    for copy in leaving:
        copy.wait()


def select(slots, table, asked):
    peers = asked.shape[0]
    chunks = slots + slots // 2 + 1
    whole = pl.BlockSpec(memory_space=pltpu.VMEM)
    return pl.pallas_call(
        functools.partial(select_kernel, slots),
        out_shape=jax.ShapeDtypeStruct((peers, 2 * chunks, LANES), BF16),
        in_specs=[whole, whole],
        out_specs=pl.BlockSpec(memory_space=pl.ANY),
        scratch_shapes=[
            pltpu.VMEM((peers, 2 * chunks, LANES), F32),
            pltpu.VMEM((peers, 2 * chunks, LANES), BF16),
            pltpu.SemaphoreType.DMA((4,)),
        ],
        compiler_params=pltpu.CompilerParams(vmem_limit_bytes=24 << 20),
        name="select_pieces",
    )(table, asked)


def contract_kernel(depth, columns, me_ref, a_ref, *refs):
    parts, out_ref, tails = refs[:-2], refs[-2], refs[-1]
    ring = len(parts)
    chunks = a_ref.shape[0] // 2
    slabs = columns // LANES
    left = columns - slabs * LANES
    halves = [jnp.concatenate([a_ref[r * chunks + j] for j in range(chunks)], axis=1) for r in range(2)]
    a = jnp.concatenate(halves, axis=0)
    tails[...] = jnp.zeros_like(tails)
    for step, part in enumerate(parts):
        p = jnp.bitwise_xor(me_ref[0], PLACES[step])
        wide = jnp.concatenate([part[s * depth : (s + 1) * depth, :] for s in range(slabs)], axis=1)
        product = jnp.dot(a[:, :depth], wide, preferred_element_type=F32).astype(BF16)
        for s in range(slabs):
            out_ref[slabs * p + s] = product[:, s * LANES : (s + 1) * LANES]
        narrow = [part[at : at + left, :] for at in range(slabs * depth, part.shape[0], left)]
        tails[pl.ds(pl.multiple_of(p * left, left), left), :] = jnp.concatenate(narrow, axis=1)
    last = lax.dot_general(a, tails[...], (((1,), (1,)), ((), ())), preferred_element_type=F32)
    out_ref[out_ref.shape[0] - 1] = last.astype(BF16)


def contract(depth, columns, me, arrived, parts):
    ring = len(parts)
    chunks2, peers, _ = arrived.shape
    outs = ring * (columns // LANES) + 1
    whole = pl.BlockSpec(memory_space=pltpu.VMEM)
    return pl.pallas_call(
        functools.partial(contract_kernel, depth, columns),
        out_shape=jax.ShapeDtypeStruct((outs, 2 * peers, LANES), BF16),
        in_specs=[pl.BlockSpec(memory_space=pltpu.SMEM)] + [whole] * (1 + ring),
        out_specs=whole,
        scratch_shapes=[pltpu.VMEM((LANES, chunks2 // 2 * LANES), BF16)],
        compiler_params=pltpu.CompilerParams(vmem_limit_bytes=24 << 20),
        name="contract",
    )(me, arrived, *parts)


def place_kernel(columns, sizes, r_ref, out_ref):
    count, blocks, _ = r_ref.shape
    slabs = columns // LANES
    left = columns - slabs * LANES
    came = lax.broadcasted_iota(jnp.int32, (blocks, blocks), 0)
    goes = lax.broadcasted_iota(jnp.int32, (blocks, blocks), 1)
    order, rest = jnp.zeros_like(came), came
    for axis in reversed(("core", *SERVED)):
        order += rest % sizes[axis] * math.prod(sizes[a] for a in TILE[TILE.index(axis) + 1 :])
        rest = rest // sizes[axis]
    turn = (order == goes).astype(F32).astype(BF16)
    for j in range(count):
        block = lax.dot_general(r_ref[j], turn, (((0,), (0,)), ((), ())), preferred_element_type=F32).astype(BF16)
        if j < count - 1:
            at = j // slabs * columns + j % slabs * LANES
            out_ref[at : at + LANES, :] = block
        else:
            for p in range((count - 1) // slabs):
                at = p * columns + slabs * LANES
                out_ref[at : at + left, :] = block[p * left : (p + 1) * left]


def place(columns, sizes, received):
    count, blocks, _ = received.shape
    ring = (count - 1) // (columns // LANES)
    whole = pl.BlockSpec(memory_space=pltpu.VMEM)
    return pl.pallas_call(
        functools.partial(place_kernel, columns, sizes),
        out_shape=jax.ShapeDtypeStruct((ring * columns, blocks), BF16),
        in_specs=[whole],
        out_specs=whole,
        compiler_params=pltpu.CompilerParams(vmem_limit_bytes=24 << 20),
        name="place_rows",
    )(received)


def local(amplitudes, integrals, tile_column, block_symmetry):
    window, _, virtuals = amplitudes.shape
    slots, width, columns = integrals.shape
    depth = slots * width
    ring = lax.axis_size("pair")
    sizes = {axis: lax.axis_size(axis) for axis in TILE}
    peers = math.prod(sizes[axis] for axis in SERVED)

    packed, wanted = pack(window, peers, integrals, tile_column, block_symmetry)
    asked = lax.all_to_all(wanted, SERVED, 0, 0, tiled=True)
    own = amplitudes.reshape(window, virtuals)
    other = lax.ppermute(own, "core", [(0, 1), (1, 0)])
    table = build_table(lax.axis_index("core").reshape(1), own, other)
    parts = [packed]
    parts += [lax.ppermute(packed, "pair", [(i ^ k, i) for i in range(ring)]) for k in PLACES[1:]]

    outgoing = select(slots, table, asked)
    arrived = jnp.transpose(lax.all_to_all(outgoing, SERVED, 0, 0, tiled=True), (1, 0, 2))
    rows = contract(depth, columns, lax.axis_index("pair").reshape(1), arrived, parts)
    received = lax.all_to_all(rows, ("core", *SERVED), 1, 1, tiled=True)
    return place(columns, sizes, received).T[None]


def solution(mesh):
    cut = {8: (1, 1, 2, 1, 1, 2, 2), 16: (1, 2, 2, 1, 1, 2, 2), 128: (2,) * 7}[mesh.shape["tile"]]
    fine = Mesh(mesh.devices.reshape(*cut, mesh.shape["pair"]), (*TILE, "pair"))
    in_specs = (P(None, (*TILE, "pair"), None), P(TILE, None, "pair"), P(TILE), P(TILE))
    out_specs = P((*TILE, "pair"), None, None)
    return jax.shard_map(local, mesh=fine, in_specs=in_specs, out_specs=out_specs, check_vma=False)
```

```python
import functools
import math

import jax
import jax.numpy as jnp
from jax import lax
from jax.experimental import pallas as pl
from jax.experimental.pallas import tpu as pltpu
from jax.sharding import Mesh, PartitionSpec as P

LANES = 128
BF16 = jnp.bfloat16
F32 = jnp.float32

HEAD = 128
MIDDLE = 64
LAST = 8

TILE = ("y4", "y2", "y1", "z4", "z2", "z1", "core")
SERVED = ("y1", "y2", "y4", "z1", "z2", "z4")

PLACES = (0, 1, 2, 3)


def pack_kernel(window, w_hbm, column_hbm, symmetry_hbm, out_hbm, ask_hbm, w_ref, column_ref, symmetry_ref, out_ref, ask_ref, arrivals, departures):
    slots, width, columns = w_ref.shape
    scalars = [
        pltpu.make_async_copy(column_hbm, column_ref, arrivals.at[slots]),
        pltpu.make_async_copy(symmetry_hbm, symmetry_ref, arrivals.at[slots + 1]),
    ]
    tiles = [pltpu.make_async_copy(w_hbm.at[k], w_ref.at[k], arrivals.at[k]) for k in range(slots)]
    for copy in scalars + tiles:
        copy.start()

    for copy in scalars:
        copy.wait()
    peers, tile, _ = ask_ref.shape
    lanes = lax.broadcasted_iota(jnp.int32, (tile, LANES), 1)
    row = jnp.zeros((tile, LANES), F32)
    for k in range(slots):
        column = column_ref[k]
        irrep = sum((column >= h * (window // 4)).astype(jnp.int32) for h in (1, 2, 3))
        place = jnp.bitwise_xor(symmetry_ref[0], irrep) * window + column
        row = jnp.where(lanes == k, place.astype(F32), row)
    row = row.astype(BF16)
    for j in range(peers):
        ask_ref[j] = row
    leaving = [pltpu.make_async_copy(ask_ref, ask_hbm, departures.at[0])]
    leaving[0].start()

    depth = slots * width
    slabs = columns // LANES
    left = columns - slabs * LANES
    for k in range(slots):
        tiles[k].wait()
        for s in range(slabs):
            lo, hi = s * LANES, (s + 1) * LANES
            at = s * depth + k * HEAD
            out_ref[at : at + HEAD, :] = w_ref[k, :HEAD, lo:hi]
            at = s * depth + slots * HEAD + k * MIDDLE
            out_ref[at : at + MIDDLE, :] = w_ref[k, HEAD : HEAD + MIDDLE, lo:hi]

    def ends(lo, hi):
        return jnp.concatenate([w_ref[k, HEAD + MIDDLE :, lo:hi].astype(F32) for k in range(slots)], axis=0).astype(BF16)

    for s in range(slabs):
        at = s * depth + slots * (HEAD + MIDDLE)
        out_ref[at : at + slots * LAST, :] = ends(s * LANES, (s + 1) * LANES)
        rows = pl.ds(s * depth, depth)
        leaving.append(pltpu.make_async_copy(out_ref.at[rows], out_hbm.at[rows], departures.at[1 + s]))
        leaving[-1].start()
    lo, hi = slabs * LANES, columns
    narrow = [w_ref[k, :HEAD, lo:hi] for k in range(slots)]
    narrow += [w_ref[k, HEAD : HEAD + MIDDLE, lo:hi] for k in range(slots)]
    narrow = jnp.concatenate(narrow + [ends(lo, hi)], axis=0)
    eye = (
        lax.broadcasted_iota(jnp.int32, (left, left), 0) == lax.broadcasted_iota(jnp.int32, (left, left), 1)
    ).astype(BF16)
    turned = lax.dot_general(eye, narrow, (((1,), (1,)), ((), ())), preferred_element_type=F32)
    chunks = -(-depth // LANES)
    turned = jnp.concatenate([turned, jnp.zeros((left, chunks * LANES - depth), F32)], axis=1).astype(BF16)
    for j in range(chunks):
        at = slabs * depth + j * left
        out_ref[at : at + left, :] = turned[:, j * LANES : (j + 1) * LANES]
    rows = pl.ds(slabs * depth, chunks * left)
    leaving.append(pltpu.make_async_copy(out_ref.at[rows], out_hbm.at[rows], departures.at[1 + slabs]))
    leaving[-1].start()
    for copy in leaving:
        copy.wait()


def pack(window, peers, integrals, tile_column, block_symmetry):
    slots, width, columns = integrals.shape
    slabs = columns // LANES
    left = columns - slabs * LANES
    depth = slots * width
    rows = slabs * depth + -(-depth // LANES) * left
    anywhere = pl.BlockSpec(memory_space=pl.ANY)
    return pl.pallas_call(
        functools.partial(pack_kernel, window),
        out_shape=[
            jax.ShapeDtypeStruct((rows, LANES), BF16),
            jax.ShapeDtypeStruct((peers, 8, LANES), BF16),
        ],
        in_specs=[anywhere, anywhere, anywhere],
        out_specs=[anywhere, anywhere],
        scratch_shapes=[
            pltpu.VMEM(integrals.shape, BF16),
            pltpu.SMEM(tile_column.shape, jnp.int32),
            pltpu.SMEM(block_symmetry.shape, jnp.int32),
            pltpu.VMEM((rows, LANES), BF16),
            pltpu.VMEM((peers, 8, LANES), BF16),
            pltpu.SemaphoreType.DMA((slots + 2,)),
            pltpu.SemaphoreType.DMA((slabs + 2,)),
        ],
        compiler_params=pltpu.CompilerParams(vmem_limit_bytes=60 << 20),
        name="pack_integrals",
    )(integrals, tile_column, block_symmetry)


def table_kernel(core_ref, own_ref, other_ref, out_ref):
    window, virtuals = own_ref.shape
    width = virtuals // 4
    first = core_ref[0] == 0
    own = own_ref[...].astype(F32)
    other = other_ref[...].astype(F32)
    rows = [jnp.where(first, own, other), jnp.where(first, other, own)]
    blank = jnp.zeros((4 * window, 2 * LANES - width), F32)
    quarters = [jnp.concatenate([row[:, h * width : (h + 1) * width] for h in range(4)], axis=0) for row in rows]
    out_ref[...] = jnp.concatenate([quarters[0], blank, quarters[1], blank], axis=1).astype(BF16)


def build_table(core, own, other):
    whole = pl.BlockSpec(memory_space=pltpu.VMEM)
    return pl.pallas_call(
        table_kernel,
        out_shape=jax.ShapeDtypeStruct((4 * own.shape[0], 4 * LANES), BF16),
        in_specs=[pl.BlockSpec(memory_space=pltpu.SMEM), whole, whole],
        out_specs=whole,
        compiler_params=pltpu.CompilerParams(vmem_limit_bytes=24 << 20),
        name="build_table",
    )(core, own, other)


def select_kernel(slots, table_ref, asked_ref, out_hbm, rows, narrow, departures):
    peers = asked_ref.shape[0]
    table = table_ref[...]
    wanted = asked_ref[...].astype(F32)[:, 0, :].astype(jnp.int32)
    places = lax.broadcasted_iota(jnp.int32, (peers, table.shape[0]), 1)
    pieces = []
    for k in range(slots):
        chosen = (places == wanted[:, k : k + 1]).astype(F32).astype(BF16)
        pieces.append(jnp.dot(chosen, table, preferred_element_type=F32))
    chunks = slots + slots // 2 + 1
    for r in range(2):
        base = r * 2 * LANES
        for k in range(slots):
            rows[:, r * chunks + k, :] = pieces[k][:, base : base + LANES]
        for j in range(slots // 2):
            lo, hi = base + HEAD, base + HEAD + MIDDLE
            pair = [pieces[2 * j][:, lo:hi], pieces[2 * j + 1][:, lo:hi]]
            rows[:, r * chunks + slots + j, :] = jnp.concatenate(pair, axis=1)
        lo = base + HEAD + MIDDLE
        ends = [pieces[k][:, lo : lo + LAST] for k in range(slots)]
        ends.append(jnp.zeros((peers, LANES - slots * LAST), F32))
        rows[:, r * chunks + chunks - 1, :] = jnp.concatenate(ends, axis=1)
    count = departures.shape[0]
    leaving = []
    for k in range(count):
        group = pl.ds(k * (peers // count), peers // count)
        narrow[group] = rows[group].astype(BF16)
        leaving.append(pltpu.make_async_copy(narrow.at[group], out_hbm.at[group], departures.at[k]))
        leaving[-1].start()
    for copy in leaving:
        copy.wait()


def select(slots, table, asked):
    peers = asked.shape[0]
    chunks = slots + slots // 2 + 1
    whole = pl.BlockSpec(memory_space=pltpu.VMEM)
    return pl.pallas_call(
        functools.partial(select_kernel, slots),
        out_shape=jax.ShapeDtypeStruct((peers, 2 * chunks, LANES), BF16),
        in_specs=[whole, whole],
        out_specs=pl.BlockSpec(memory_space=pl.ANY),
        scratch_shapes=[
            pltpu.VMEM((peers, 2 * chunks, LANES), F32),
            pltpu.VMEM((peers, 2 * chunks, LANES), BF16),
            pltpu.SemaphoreType.DMA((4,)),
        ],
        compiler_params=pltpu.CompilerParams(vmem_limit_bytes=24 << 20),
        name="select_pieces",
    )(table, asked)


def contract_kernel(depth, columns, steps, me_ref, a_ref, *refs):
    parts, earlier, out_ref, tails = refs[: len(steps)], refs[len(steps) : -2], refs[-2], refs[-1]
    chunks = a_ref.shape[0] // 2
    slabs = columns // LANES
    left = columns - slabs * LANES
    halves = [jnp.concatenate([a_ref[r * chunks + j] for j in range(chunks)], axis=1) for r in range(2)]
    a = jnp.concatenate(halves, axis=0)
    tails[...] = jnp.zeros_like(tails)
    for before in earlier:
        out_ref[...] = before[...]
    for step, part in zip(steps, parts):
        p = jnp.bitwise_xor(me_ref[0], step)
        wide = jnp.concatenate([part[s * depth : (s + 1) * depth, :] for s in range(slabs)], axis=1)
        product = jnp.dot(a[:, :depth], wide, preferred_element_type=F32).astype(BF16)
        for s in range(slabs):
            out_ref[slabs * p + s] = product[:, s * LANES : (s + 1) * LANES]
        narrow = [part[at : at + left, :] for at in range(slabs * depth, part.shape[0], left)]
        tails[pl.ds(pl.multiple_of(p * left, left), left), :] = jnp.concatenate(narrow, axis=1)
    last = lax.dot_general(a, tails[...], (((1,), (1,)), ((), ())), preferred_element_type=F32)
    for before in earlier:
        last = last + before[before.shape[0] - 1].astype(F32)
    out_ref[out_ref.shape[0] - 1] = last.astype(BF16)


def contract(depth, columns, ring, me, arrived, steps, parts, earlier=()):
    chunks2, peers, _ = arrived.shape
    outs = ring * (columns // LANES) + 1
    whole = pl.BlockSpec(memory_space=pltpu.VMEM)
    return pl.pallas_call(
        functools.partial(contract_kernel, depth, columns, steps),
        out_shape=jax.ShapeDtypeStruct((outs, 2 * peers, LANES), BF16),
        in_specs=[pl.BlockSpec(memory_space=pltpu.SMEM)] + [whole] * (1 + len(parts) + len(earlier)),
        out_specs=whole,
        scratch_shapes=[pltpu.VMEM((LANES, chunks2 // 2 * LANES), BF16)],
        compiler_params=pltpu.CompilerParams(vmem_limit_bytes=24 << 20),
        name="contract",
    )(me, arrived, *parts, *earlier)


def place_kernel(columns, sizes, r_ref, out_ref):
    count, blocks, _ = r_ref.shape
    slabs = columns // LANES
    left = columns - slabs * LANES
    came = lax.broadcasted_iota(jnp.int32, (blocks, blocks), 0)
    goes = lax.broadcasted_iota(jnp.int32, (blocks, blocks), 1)
    order, rest = jnp.zeros_like(came), came
    for axis in reversed(("core", *SERVED)):
        order += rest % sizes[axis] * math.prod(sizes[a] for a in TILE[TILE.index(axis) + 1 :])
        rest = rest // sizes[axis]
    turn = (order == goes).astype(F32).astype(BF16)
    for j in range(count):
        block = lax.dot_general(r_ref[j], turn, (((0,), (0,)), ((), ())), preferred_element_type=F32).astype(BF16)
        if j < count - 1:
            at = j // slabs * columns + j % slabs * LANES
            out_ref[at : at + LANES, :] = block
        else:
            for p in range((count - 1) // slabs):
                at = p * columns + slabs * LANES
                out_ref[at : at + left, :] = block[p * left : (p + 1) * left]


def place(columns, sizes, received):
    count, blocks, _ = received.shape
    ring = (count - 1) // (columns // LANES)
    whole = pl.BlockSpec(memory_space=pltpu.VMEM)
    return pl.pallas_call(
        functools.partial(place_kernel, columns, sizes),
        out_shape=jax.ShapeDtypeStruct((ring * columns, blocks), BF16),
        in_specs=[whole],
        out_specs=whole,
        compiler_params=pltpu.CompilerParams(vmem_limit_bytes=24 << 20),
        name="place_rows",
    )(received)


def local(amplitudes, integrals, tile_column, block_symmetry):
    window, _, virtuals = amplitudes.shape
    slots, width, columns = integrals.shape
    depth = slots * width
    ring = lax.axis_size("pair")
    sizes = {axis: lax.axis_size(axis) for axis in TILE}
    peers = math.prod(sizes[axis] for axis in SERVED)

    packed, wanted = pack(window, peers, integrals, tile_column, block_symmetry)
    asked = lax.all_to_all(wanted, SERVED, 0, 0, tiled=True)
    own = amplitudes.reshape(window, virtuals)
    other = lax.ppermute(own, "core", [(0, 1), (1, 0)])
    table = build_table(lax.axis_index("core").reshape(1), own, other)
    parts = [packed]
    parts += [lax.ppermute(packed, "pair", [(i ^ k, i) for i in range(ring)]) for k in PLACES[1:]]

    outgoing = select(slots, table, asked)
    arrived = jnp.transpose(lax.all_to_all(outgoing, SERVED, 0, 0, tiled=True), (1, 0, 2))
    here = lax.axis_index("pair").reshape(1)
    rows = contract(depth, columns, ring, here, arrived, (PLACES[0], PLACES[3]), [parts[0], parts[3]])
    rows = contract(depth, columns, ring, here, arrived, PLACES[1:3], parts[1:3], (rows,))
    received = lax.all_to_all(rows, ("core", *SERVED), 1, 1, tiled=True)
    return place(columns, sizes, received).T[None]


def solution(mesh):
    cut = {8: (1, 1, 2, 1, 1, 2, 2), 16: (1, 2, 2, 1, 1, 2, 2), 128: (2,) * 7}[mesh.shape["tile"]]
    fine = Mesh(mesh.devices.reshape(*cut, mesh.shape["pair"]), (*TILE, "pair"))
    in_specs = (P(None, (*TILE, "pair"), None), P(TILE, None, "pair"), P(TILE), P(TILE))
    out_specs = P((*TILE, "pair"), None, None)
    return jax.shard_map(local, mesh=fine, in_specs=in_specs, out_specs=out_specs, check_vma=False)
```

```python
import functools
import math

import jax
import jax.numpy as jnp
from jax import lax
from jax.experimental import pallas as pl
from jax.experimental.pallas import tpu as pltpu
from jax.sharding import Mesh, PartitionSpec as P

LANES = 128
BF16 = jnp.bfloat16
F32 = jnp.float32

HEAD = 128
MIDDLE = 64
LAST = 8

TILE = ("y4", "y2", "y1", "z4", "z2", "z1", "core")
SERVED = ("y1", "y2", "y4", "z1", "z2", "z4")

PLACES = (0, 1, 2, 3)


def pack_kernel(window, w_hbm, column_hbm, symmetry_hbm, out_hbm, ask_hbm, w_ref, column_ref, symmetry_ref, out_ref, ask_ref, arrivals, departures):
    slots, width, columns = w_ref.shape
    scalars = [
        pltpu.make_async_copy(column_hbm, column_ref, arrivals.at[slots]),
        pltpu.make_async_copy(symmetry_hbm, symmetry_ref, arrivals.at[slots + 1]),
    ]
    tiles = [pltpu.make_async_copy(w_hbm.at[k], w_ref.at[k], arrivals.at[k]) for k in range(slots)]
    for copy in scalars + tiles:
        copy.start()

    for copy in scalars:
        copy.wait()
    peers, tile, _ = ask_ref.shape
    lanes = lax.broadcasted_iota(jnp.int32, (tile, LANES), 1)
    row = jnp.zeros((tile, LANES), F32)
    for k in range(slots):
        column = column_ref[k]
        irrep = sum((column >= h * (window // 4)).astype(jnp.int32) for h in (1, 2, 3))
        place = jnp.bitwise_xor(symmetry_ref[0], irrep) * window + column
        row = jnp.where(lanes == k, place.astype(F32), row)
    row = row.astype(BF16)
    for j in range(peers):
        ask_ref[j] = row
    leaving = [pltpu.make_async_copy(ask_ref, ask_hbm, departures.at[0])]
    leaving[0].start()

    depth = slots * width
    slabs = columns // LANES
    left = columns - slabs * LANES
    for k in range(slots):
        tiles[k].wait()
        for s in range(slabs):
            lo, hi = s * LANES, (s + 1) * LANES
            at = s * depth + k * HEAD
            out_ref[at : at + HEAD, :] = w_ref[k, :HEAD, lo:hi]
            at = s * depth + slots * HEAD + k * MIDDLE
            out_ref[at : at + MIDDLE, :] = w_ref[k, HEAD : HEAD + MIDDLE, lo:hi]

    def ends(lo, hi):
        return jnp.concatenate([w_ref[k, HEAD + MIDDLE :, lo:hi].astype(F32) for k in range(slots)], axis=0).astype(BF16)

    for s in range(slabs):
        at = s * depth + slots * (HEAD + MIDDLE)
        out_ref[at : at + slots * LAST, :] = ends(s * LANES, (s + 1) * LANES)
        rows = pl.ds(s * depth, depth)
        leaving.append(pltpu.make_async_copy(out_ref.at[rows], out_hbm.at[rows], departures.at[1 + s]))
        leaving[-1].start()
    lo, hi = slabs * LANES, columns
    narrow = [w_ref[k, :HEAD, lo:hi] for k in range(slots)]
    narrow += [w_ref[k, HEAD : HEAD + MIDDLE, lo:hi] for k in range(slots)]
    narrow = jnp.concatenate(narrow + [ends(lo, hi)], axis=0)
    eye = (
        lax.broadcasted_iota(jnp.int32, (left, left), 0) == lax.broadcasted_iota(jnp.int32, (left, left), 1)
    ).astype(BF16)
    turned = lax.dot_general(eye, narrow, (((1,), (1,)), ((), ())), preferred_element_type=F32)
    chunks = -(-depth // LANES)
    turned = jnp.concatenate([turned, jnp.zeros((left, chunks * LANES - depth), F32)], axis=1).astype(BF16)
    for j in range(chunks):
        at = slabs * depth + j * left
        out_ref[at : at + left, :] = turned[:, j * LANES : (j + 1) * LANES]
    rows = pl.ds(slabs * depth, chunks * left)
    leaving.append(pltpu.make_async_copy(out_ref.at[rows], out_hbm.at[rows], departures.at[1 + slabs]))
    leaving[-1].start()
    for copy in leaving:
        copy.wait()


def pack(window, peers, integrals, tile_column, block_symmetry):
    slots, width, columns = integrals.shape
    slabs = columns // LANES
    left = columns - slabs * LANES
    depth = slots * width
    rows = slabs * depth + -(-depth // LANES) * left
    anywhere = pl.BlockSpec(memory_space=pl.ANY)
    return pl.pallas_call(
        functools.partial(pack_kernel, window),
        out_shape=[
            jax.ShapeDtypeStruct((rows, LANES), BF16),
            jax.ShapeDtypeStruct((peers, 4, LANES), BF16),
        ],
        in_specs=[anywhere, anywhere, anywhere],
        out_specs=[anywhere, anywhere],
        scratch_shapes=[
            pltpu.VMEM(integrals.shape, BF16),
            pltpu.SMEM(tile_column.shape, jnp.int32),
            pltpu.SMEM(block_symmetry.shape, jnp.int32),
            pltpu.VMEM((rows, LANES), BF16),
            pltpu.VMEM((peers, 4, LANES), BF16),
            pltpu.SemaphoreType.DMA((slots + 2,)),
            pltpu.SemaphoreType.DMA((slabs + 2,)),
        ],
        compiler_params=pltpu.CompilerParams(vmem_limit_bytes=60 << 20),
        name="pack_integrals",
    )(integrals, tile_column, block_symmetry)


def table_kernel(core_ref, own_ref, other_ref, out_ref):
    window, virtuals = own_ref.shape
    width = virtuals // 4
    first = core_ref[0] == 0
    own = own_ref[...].astype(F32)
    other = other_ref[...].astype(F32)
    rows = [jnp.where(first, own, other), jnp.where(first, other, own)]
    blank = jnp.zeros((4 * window, 2 * LANES - width), F32)
    quarters = [jnp.concatenate([row[:, h * width : (h + 1) * width] for h in range(4)], axis=0) for row in rows]
    out_ref[...] = jnp.concatenate([quarters[0], blank, quarters[1], blank], axis=1).astype(BF16)


def build_table(core, own, other):
    whole = pl.BlockSpec(memory_space=pltpu.VMEM)
    return pl.pallas_call(
        table_kernel,
        out_shape=jax.ShapeDtypeStruct((4 * own.shape[0], 4 * LANES), BF16),
        in_specs=[pl.BlockSpec(memory_space=pltpu.SMEM), whole, whole],
        out_specs=whole,
        compiler_params=pltpu.CompilerParams(vmem_limit_bytes=24 << 20),
        name="build_table",
    )(core, own, other)


def select_kernel(slots, table_ref, asked_ref, out_hbm, rows, narrow, departures):
    peers = asked_ref.shape[0]
    table = table_ref[...]
    wanted = asked_ref[...].astype(F32)[:, 0, :].astype(jnp.int32)
    places = lax.broadcasted_iota(jnp.int32, (peers, table.shape[0]), 1)
    pieces = []
    for k in range(slots):
        chosen = (places == wanted[:, k : k + 1]).astype(F32).astype(BF16)
        pieces.append(jnp.dot(chosen, table, preferred_element_type=F32))
    chunks = slots + slots // 2 + 1
    for r in range(2):
        base = r * 2 * LANES
        for k in range(slots):
            rows[:, r * chunks + k, :] = pieces[k][:, base : base + LANES]
        for j in range(slots // 2):
            lo, hi = base + HEAD, base + HEAD + MIDDLE
            pair = [pieces[2 * j][:, lo:hi], pieces[2 * j + 1][:, lo:hi]]
            rows[:, r * chunks + slots + j, :] = jnp.concatenate(pair, axis=1)
        lo = base + HEAD + MIDDLE
        ends = [pieces[k][:, lo : lo + LAST] for k in range(slots)]
        ends.append(jnp.zeros((peers, LANES - slots * LAST), F32))
        rows[:, r * chunks + chunks - 1, :] = jnp.concatenate(ends, axis=1)
    count = departures.shape[0]
    leaving = []
    for k in range(count):
        group = pl.ds(k * (peers // count), peers // count)
        narrow[group] = rows[group].astype(BF16)
        leaving.append(pltpu.make_async_copy(narrow.at[group], out_hbm.at[group], departures.at[k]))
        leaving[-1].start()
    for copy in leaving:
        copy.wait()


def select(slots, table, asked):
    peers = asked.shape[0]
    chunks = slots + slots // 2 + 1
    whole = pl.BlockSpec(memory_space=pltpu.VMEM)
    return pl.pallas_call(
        functools.partial(select_kernel, slots),
        out_shape=jax.ShapeDtypeStruct((peers, 2 * chunks, LANES), BF16),
        in_specs=[whole, whole],
        out_specs=pl.BlockSpec(memory_space=pl.ANY),
        scratch_shapes=[
            pltpu.VMEM((peers, 2 * chunks, LANES), F32),
            pltpu.VMEM((peers, 2 * chunks, LANES), BF16),
            pltpu.SemaphoreType.DMA((4,)),
        ],
        compiler_params=pltpu.CompilerParams(vmem_limit_bytes=24 << 20),
        name="select_pieces",
    )(table, asked)


def contract_kernel(depth, columns, me_ref, a_ref, *refs):
    parts, out_ref, tails = refs[:-2], refs[-2], refs[-1]
    ring = len(parts)
    chunks = a_ref.shape[0] // 2
    slabs = columns // LANES
    left = columns - slabs * LANES
    halves = [jnp.concatenate([a_ref[r * chunks + j] for j in range(chunks)], axis=1) for r in range(2)]
    a = jnp.concatenate(halves, axis=0)
    tails[...] = jnp.zeros_like(tails)
    for step, part in enumerate(parts):
        p = jnp.bitwise_xor(me_ref[0], PLACES[step])
        wide = jnp.concatenate([part[s * depth : (s + 1) * depth, :] for s in range(slabs)], axis=1)
        product = jnp.dot(a[:, :depth], wide, preferred_element_type=F32).astype(BF16)
        for s in range(slabs):
            out_ref[slabs * p + s] = product[:, s * LANES : (s + 1) * LANES]
        narrow = [part[at : at + left, :] for at in range(slabs * depth, part.shape[0], left)]
        tails[pl.ds(pl.multiple_of(p * left, left), left), :] = jnp.concatenate(narrow, axis=1)
    last = lax.dot_general(a, tails[...], (((1,), (1,)), ((), ())), preferred_element_type=F32)
    out_ref[out_ref.shape[0] - 1] = last.astype(BF16)


def contract(depth, columns, me, arrived, parts):
    ring = len(parts)
    chunks2, peers, _ = arrived.shape
    outs = ring * (columns // LANES) + 1
    whole = pl.BlockSpec(memory_space=pltpu.VMEM)
    return pl.pallas_call(
        functools.partial(contract_kernel, depth, columns),
        out_shape=jax.ShapeDtypeStruct((outs, 2 * peers, LANES), BF16),
        in_specs=[pl.BlockSpec(memory_space=pltpu.SMEM)] + [whole] * (1 + ring),
        out_specs=whole,
        scratch_shapes=[pltpu.VMEM((LANES, chunks2 // 2 * LANES), BF16)],
        compiler_params=pltpu.CompilerParams(vmem_limit_bytes=24 << 20),
        name="contract",
    )(me, arrived, *parts)


def place_kernel(columns, sizes, r_ref, out_ref):
    count, blocks, _ = r_ref.shape
    slabs = columns // LANES
    left = columns - slabs * LANES
    came = lax.broadcasted_iota(jnp.int32, (blocks, blocks), 0)
    goes = lax.broadcasted_iota(jnp.int32, (blocks, blocks), 1)
    order, rest = jnp.zeros_like(came), came
    for axis in reversed(("core", *SERVED)):
        order += rest % sizes[axis] * math.prod(sizes[a] for a in TILE[TILE.index(axis) + 1 :])
        rest = rest // sizes[axis]
    turn = (order == goes).astype(F32).astype(BF16)
    for j in range(count):
        block = lax.dot_general(r_ref[j], turn, (((0,), (0,)), ((), ())), preferred_element_type=F32).astype(BF16)
        if j < count - 1:
            at = j // slabs * columns + j % slabs * LANES
            out_ref[at : at + LANES, :] = block
        else:
            for p in range((count - 1) // slabs):
                at = p * columns + slabs * LANES
                out_ref[at : at + left, :] = block[p * left : (p + 1) * left]


def place(columns, sizes, received):
    count, blocks, _ = received.shape
    ring = (count - 1) // (columns // LANES)
    whole = pl.BlockSpec(memory_space=pltpu.VMEM)
    return pl.pallas_call(
        functools.partial(place_kernel, columns, sizes),
        out_shape=jax.ShapeDtypeStruct((ring * columns, blocks), BF16),
        in_specs=[whole],
        out_specs=whole,
        compiler_params=pltpu.CompilerParams(vmem_limit_bytes=24 << 20),
        name="place_rows",
    )(received)


def local(amplitudes, integrals, tile_column, block_symmetry):
    window, _, virtuals = amplitudes.shape
    slots, width, columns = integrals.shape
    depth = slots * width
    ring = lax.axis_size("pair")
    sizes = {axis: lax.axis_size(axis) for axis in TILE}
    peers = math.prod(sizes[axis] for axis in SERVED)

    packed, wanted = pack(window, peers, integrals, tile_column, block_symmetry)
    asked = lax.all_to_all(wanted, SERVED, 0, 0, tiled=True)
    own = amplitudes.reshape(window, virtuals)
    other = lax.ppermute(own, "core", [(0, 1), (1, 0)])
    table = build_table(lax.axis_index("core").reshape(1), own, other)
    parts = [packed]
    parts += [lax.ppermute(packed, "pair", [(i ^ k, i) for i in range(ring)]) for k in PLACES[1:]]

    outgoing = select(slots, table, asked)
    arrived = jnp.transpose(lax.all_to_all(outgoing, SERVED, 0, 0, tiled=True), (1, 0, 2))
    rows = contract(depth, columns, lax.axis_index("pair").reshape(1), arrived, parts)
    received = lax.all_to_all(rows, ("core", *SERVED), 1, 1, tiled=True)
    return place(columns, sizes, received).T[None]


def solution(mesh):
    cut = {8: (1, 1, 2, 1, 1, 2, 2), 16: (1, 2, 2, 1, 1, 2, 2), 128: (2,) * 7}[mesh.shape["tile"]]
    fine = Mesh(mesh.devices.reshape(*cut, mesh.shape["pair"]), (*TILE, "pair"))
    in_specs = (P(None, (*TILE, "pair"), None), P(TILE, None, "pair"), P(TILE), P(TILE))
    out_specs = P((*TILE, "pair"), None, None)
    return jax.shard_map(local, mesh=fine, in_specs=in_specs, out_specs=out_specs, check_vma=False)
```
